32 devices in a mesh: dp: 8 (over z, x), mp: 4 (over y, core).
Axes of the slice: x: 2, y: 2, z: 4, core: 2. Of those that a mesh axis runs over, the one named last changes fastest.
Arguments:
- inputs: bfloat16 [2, 1024, 1024], P(None, 'dp'), may hold values from -6 to 6
- segment: int32 [2, 1024], P(None, 'dp'), may hold values from 0 to 15, never falling along the last dimension, each value on 1 to 128 neighbouring positions
- norm_gain: bfloat16 [1024], P(('dp', 'mp')), may hold values from 0.5 to 1.5
- w_query: bfloat16 [1024, 512], P('dp', 'mp'), may hold values from -0.1875 to 0.1875
- w_key: bfloat16 [1024, 512], P('dp', 'mp'), may hold values from -0.1875 to 0.1875
- w_value: bfloat16 [1024, 1024], P('dp', 'mp'), may hold values from -0.1875 to 0.1875
- w_gate_out: bfloat16 [1024, 1024], P('dp', 'mp'), may hold values from -0.1875 to 0.1875
- w_rank_in: bfloat16 [1024, 16], P(('dp', 'mp')), may hold values from -0.1875 to 0.1875
- w_rank_out: bfloat16 [512, 16], P(('dp', 'mp')), may hold values from -1.5 to 1.5
- rank_bias: bfloat16 [512], P(('dp', 'mp')), may hold values from -2 to 5
- head_gain: bfloat16 [256], P(('dp', 'mp')), may hold values from 0.5 to 1.5
- w_output: bfloat16 [1024, 1024], P('dp', 'mp'), may hold values from -0.375 to 0.375
- ffn_gain: bfloat16 [1024], P(('dp', 'mp')), may hold values from 0.5 to 1.5
- w_ffn_gate: bfloat16 [1024, 2816], P('dp', 'mp'), may hold values from -0.1875 to 0.1875
- w_ffn_up: bfloat16 [1024, 2816], P('dp', 'mp'), may hold values from -0.1875 to 0.1875
- w_ffn_down: bfloat16 [1024, 2816], P('dp', 'mp'), may hold values from -0.21875 to 0.21875
- cotangent: bfloat16 [2, 1024, 1024], P(None, 'dp'), may hold values from -6 to 6
Outputs:
- output: bfloat16 [2, 1024, 1024], P(None, 'dp')
- input_grad: float32 [2, 1024, 1024], P(None, 'dp')
- grad_norm_gain: float32 [1024], P(('dp', 'mp'))
- grad_w_query: float32 [1024, 512], P('dp', 'mp')
- grad_w_key: float32 [1024, 512], P('dp', 'mp')
- grad_w_value: float32 [1024, 1024], P('dp', 'mp')
- grad_w_gate_out: float32 [1024, 1024], P('dp', 'mp')
- grad_w_rank_in: float32 [1024, 16], P(('dp', 'mp'))
- grad_w_rank_out: float32 [512, 16], P(('dp', 'mp'))
- grad_rank_bias: float32 [512], P(('dp', 'mp'))
- grad_head_gain: float32 [256], P(('dp', 'mp'))
- grad_w_output: float32 [1024, 1024], P('dp', 'mp')
- grad_ffn_gain: float32 [1024], P(('dp', 'mp'))
- grad_w_ffn_gate: float32 [1024, 2816], P('dp', 'mp')
- grad_w_ffn_up: float32 [1024, 2816], P('dp', 'mp')
- grad_w_ffn_down: float32 [1024, 2816], P('dp', 'mp')
The draws below stay inside these ranges and needn't reach their ends.
Inputs may be any that keep to these rules, and one draw needn't show every extreme that they name: `segment`: along each micro-batch's 1024 tokens the document numbers never fall; every document has 1 to 128 tokens, and some document has exactly 128.
All inputs are finite; a program needn't handle non-finite values.
Results may differ from the reference program's by a relative error of at most 0.02.
Values may be sent and summed in bfloat16 or wider, within the bound.
A program may use at most 128 MiB of HBM per device.

```python
import math
import jax
import jax.numpy as jnp
import numpy as np
from jax import lax

D = 1024
H = 4
DK = 128
DV = 256
FF = 2816
R = 16
SPAN = 64
SEQ = 128
MICRO = 2
TOKENS = 1024
N_DP = 8


def steps_of(own_key, dims, split, smallest, top_value):
    loudness, own = 1.0, jax.random.fold_in(own_key, 6)
    for axis_at, shards_of in split:
        draws = jnp.exp(jax.random.uniform(jax.random.fold_in(own, axis_at), (shards_of,), jnp.float32, smallest / len(split), top_value / len(split)))
        loudness = loudness * jnp.repeat(draws, dims[axis_at] // shards_of).reshape([-1 if axis == axis_at else 1 for axis in range(len(dims))])
    return loudness


def length_profile(amount, total, bound, lean):
    weights = [(1 << 20) // math.isqrt(grade ** lean) + 1 for grade in range(2, amount + 1)]
    rest, counts = total - bound - (amount - 1), [1] * (amount - 1)
    while rest > 0:
        free = [i for i in range(amount - 1) if counts[i] < bound]
        mass, left = sum([weights[i] for i in free]), rest
        for i in free:
            more = min(bound - counts[i], max(1, left * weights[i] // mass), rest)
            counts[i] = counts[i] + more
            rest = rest - more
    return np.array([bound] + counts)


def uneven(own_key, amount, total, bound, slope):
    if amount == 2:
        one = jax.random.randint(own_key, (), max(1, total - bound), min(bound, total - 1) + 1)
        return jnp.stack([one, total - one])
    sizes = jnp.asarray(length_profile(amount, total, bound, slope), jnp.int32)
    pairs = (amount - 1) // 2
    giver, taker = sizes[1:1 + 2 * pairs:2], sizes[2:2 + 2 * pairs:2]
    margin = jnp.minimum(giver - 1, bound - taker)
    shifted = jax.random.randint(jax.random.fold_in(own_key, 1), (pairs,), 0, 1 << 20) % (margin + 1)
    sizes = sizes.at[1:1 + 2 * pairs:2].set(giver - shifted).at[2:2 + 2 * pairs:2].set(taker + shifted)
    return sizes[jax.random.permutation(jax.random.fold_in(own_key, 2), amount)]


def noise(rng, shape, spread, reach, pieces=(), kind=jnp.bfloat16):
    level = steps_of(rng, shape, pieces, -0.22, 0.18) if pieces else 1.0
    entries = jax.random.normal(rng, shape, jnp.float32) * spread * level
    return jnp.minimum(jnp.maximum(entries, -reach), reach).astype(kind)


def setup_inputs(seed: int = 0) -> dict:
    key_of = jax.random.split(jax.random.key(seed), 18)
    return {
        "inputs": noise(key_of[0], (MICRO, TOKENS, D), 1.0, 6.0, ((1, 8),)),
        "segment": jax.vmap(lambda own: jnp.searchsorted(jnp.cumsum(uneven(own, 2 * N_DP, TOKENS, SEQ, 1)), jnp.arange(TOKENS), side="right"))(jax.random.split(key_of[1], MICRO)).reshape((MICRO, TOKENS)).astype(jnp.int32),
        "norm_gain": jnp.clip(1.0 + 0.1 * jax.random.normal(key_of[2], (D,), jnp.float32), 0.5, 1.5).astype(jnp.bfloat16),
        "w_query": noise(key_of[3], (D, H * DK), D ** -0.5, 0.1875, ((0, 8), (1, 4))),
        "w_key": noise(key_of[4], (D, H * DK), D ** -0.5, 0.1875, ((0, 8), (1, 4))),
        "w_value": noise(key_of[5], (D, H * DV), D ** -0.5, 0.1875, ((0, 8), (1, 4))),
        "w_gate_out": noise(key_of[6], (D, H * DV), D ** -0.5, 0.1875, ((0, 8), (1, 4))),
        "w_rank_in": noise(key_of[7], (D, R), D ** -0.5, 0.1875, ((0, 32),)),
        "w_rank_out": noise(key_of[8], (H * DK, R), R ** -0.5, 1.5, ((0, 32),)),
        "rank_bias": jnp.clip(-2.0 + 7.0 * jax.random.uniform(key_of[9], (H * DK,), jnp.float32) ** steps_of(key_of[9], (H * DK,), ((0, 32),), -0.2, 0.2), -2.0, 5.0).astype(jnp.bfloat16),
        "head_gain": jnp.clip(1.0 + 0.1 * jax.random.normal(key_of[10], (DV,), jnp.float32), 0.5, 1.5).astype(jnp.bfloat16),
        "w_output": noise(key_of[11], (D, H * DV), (H * DV // 4) ** -0.5, 0.375, ((0, 8), (1, 4))),
        "ffn_gain": jnp.clip(1.0 + 0.1 * jax.random.normal(key_of[12], (D,), jnp.float32), 0.5, 1.5).astype(jnp.bfloat16),
        "w_ffn_gate": noise(key_of[13], (D, FF), D ** -0.5, 0.1875, ((0, 8), (1, 4))),
        "w_ffn_up": noise(key_of[14], (D, FF), D ** -0.5, 0.1875, ((0, 8), (1, 4))),
        "w_ffn_down": noise(key_of[15], (D, FF), (FF // 4) ** -0.5, 0.21875, ((0, 8), (1, 4))),
        "cotangent": noise(key_of[16], (MICRO, TOKENS, D), 1.0, 6.0, ((1, 8),)),
    }


@jax.custom_vjp
def low(v):
    return lax.optimization_barrier(v.astype(jnp.bfloat16)).astype(jnp.float32)

@jax.custom_vjp
def low_back(v):
    return v

def low_keep(v):
    return (low(v), None)

def low_pass(kept, grad):
    return (grad,)

def back_keep(v):
    return (v, None)

def back_low(kept, grad):
    return (low(grad),)
low.defvjp(low_keep, low_pass)
low_back.defvjp(back_keep, back_low)
norm_eps = 1e-06
head_eps = 0.1
gate_divisor = 16.0

def product(left, right):
    return jnp.dot(left, right, precision=lax.Precision.HIGHEST, preferred_element_type=jnp.float32)

def rms_gain(values, gain):
    return values * lax.rsqrt(lax.optimization_barrier(jnp.mean(values * values, axis=-1, keepdims=True)) + norm_eps) * gain

def gla_core(queries, key_in, values, decays, segment):
    length, width = queries.shape
    value_width = values.shape[1]
    blocks = length // SPAN
    scaling = width ** (-0.5)
    previous = jnp.concatenate([jnp.full((1,), -1, jnp.int32), segment[:-1].astype(jnp.int32)])
    prev_block = previous.reshape(blocks, SPAN)[:, 0]
    positions = jnp.arange(SPAN)
    causal_base = positions[:, None] >= positions[None, :]

    def block_step(carry_state, block_items):
        query_blk, key_blk, value_blk, decay_blk, seg_blk, prev_seg = block_items
        cumulative = jnp.cumsum(decay_blk, axis=0)
        causal = causal_base & (seg_blk[:, None] == seg_blk[None, :])
        query_up = query_blk * jnp.exp(cumulative)
        key_down = key_blk * jnp.exp(-cumulative)
        scores = jnp.where(causal, product(query_up, key_down.T), 0.0)
        inner_sum = product(scores, value_blk)
        carried = (seg_blk == prev_seg)[:, None]
        outer_sum = jnp.where(carried, product(query_up, carry_state), 0.0)
        final_log = cumulative[-1]
        weighted = jnp.where((seg_blk == seg_blk[-1])[:, None], key_down * jnp.exp(final_log)[None, :], 0.0)
        kept_state = jnp.where(seg_blk[-1] == prev_seg, jnp.exp(final_log)[:, None] * carry_state, 0.0)
        new_state = kept_state + product(weighted.T, value_blk)
        return (new_state, scaling * (inner_sum + outer_sum))
    start_state = jnp.zeros((width, value_width), jnp.float32)
    block_items = (queries.reshape(blocks, SPAN, width), key_in.reshape(blocks, SPAN, width), values.reshape(blocks, SPAN, value_width), decays.reshape(blocks, SPAN, width), segment.reshape(blocks, SPAN), prev_block)
    final_state, results = lax.scan(jax.checkpoint(block_step), start_state, block_items)
    return results.reshape(length, value_width)

def head_gate(core_out, gate_lin, head_gain):
    normed = core_out * lax.rsqrt(lax.optimization_barrier(jnp.mean(core_out * core_out, axis=-1, keepdims=True)) + head_eps) * head_gain
    gate_three = gate_lin.reshape(core_out.shape)
    return (normed * gate_three * jax.nn.sigmoid(gate_three)).reshape(gate_lin.shape)

def forward(params, tokens_three, segment_two):
    gain_in, w_query, w_key, w_value, w_gate_out, w_rank_in, w_rank_out, rank_bias, head_gain, w_output, gain_mid, w_ffn_gate, w_ffn_up, w_ffn_down = params
    groups, length, width = tokens_three.shape
    tokens = tokens_three.reshape(groups * length, width)
    normed_in = low(rms_gain(tokens, gain_in))
    queries = low_back(low(product(normed_in, w_query)))
    key_in = low_back(low(product(normed_in, w_key)))
    values = low_back(low(product(normed_in, w_value)))
    gate_lin = low_back(product(normed_in, w_gate_out))
    rank_act = low_back(low(product(normed_in, w_rank_in)))
    logits = low_back(product(rank_act, w_rank_out.T) + rank_bias)
    decays = jax.nn.log_sigmoid(logits) / gate_divisor

    def split_heads(array_in):
        return array_in.reshape(groups, length, H, -1)
    core_fn = jax.vmap(jax.vmap(gla_core, in_axes=(1, 1, 1, 1, None), out_axes=1), in_axes=(0, 0, 0, 0, 0))
    core_out = core_fn(split_heads(queries), split_heads(key_in), split_heads(values), split_heads(decays), segment_two).reshape(groups * length, H, -1)
    gated_out = low(head_gate(core_out, gate_lin, head_gain))
    attended = low_back(product(gated_out, w_output.T))
    middle = tokens + attended
    normed_mid = low(rms_gain(middle, gain_mid))
    gate_act = low_back(product(normed_mid, w_ffn_gate))
    up_act = low_back(product(normed_mid, w_ffn_up))
    hidden = low(jax.nn.silu(gate_act) * up_act)
    ffn_out = low_back(product(hidden, w_ffn_down.T))
    return (middle + ffn_out).reshape(groups, length, width)

def reference(inputs, segment, norm_gain, w_query, w_key, w_value, w_gate_out, w_rank_in, w_rank_out, rank_bias, head_gain, w_output, ffn_gain, w_ffn_gate, w_ffn_up, w_ffn_down, cotangent):
    params = tuple((array_in.astype(jnp.float32) for array_in in (norm_gain, w_query, w_key, w_value, w_gate_out, w_rank_in, w_rank_out, rank_bias, head_gain, w_output, ffn_gain, w_ffn_gate, w_ffn_up, w_ffn_down)))
    seq_count = MICRO * N_DP
    group_size = math.gcd(seq_count, max(1, 4096 // SEQ))
    group_count = seq_count // group_size
    tokens = inputs.astype(jnp.float32).reshape(group_count, group_size, SEQ, D)
    segs = segment.astype(jnp.int32).reshape(group_count, group_size, SEQ)
    cotangents = cotangent.astype(jnp.float32).reshape(group_count, group_size, SEQ, D)
    zero_grads = jax.tree.map(jnp.zeros_like, params)

    def group_step(totals, group_items):
        tokens_group, segs_group, cot_group = group_items

        def run_forward(param_set, tokens_in):
            return forward(param_set, tokens_in, segs_group)
        values_out, pullback = jax.vjp(run_forward, params, tokens_group)
        grad_params, grad_tokens = pullback(cot_group)
        totals = jax.tree.map(lambda total, extra: total + extra, totals, grad_params)
        return (totals, (values_out.astype(jnp.bfloat16), grad_tokens))
    totals, (outs_all, grads_all) = lax.scan(group_step, zero_grads, (tokens, segs, cotangents))
    output = outs_all.reshape(MICRO, TOKENS, D)
    input_grad = grads_all.reshape(MICRO, TOKENS, D)
    return (output, input_grad, totals[0], totals[1], totals[2], totals[3], totals[4], totals[5], totals[6], totals[7], totals[8], totals[9], totals[10], totals[11], totals[12], totals[13])
```

```python
import jax
import jax.numpy as jnp
from jax import lax
from jax.sharding import PartitionSpec as P

H = 4
norm_eps = 1e-06
head_eps = 0.1
gate_divisor = 16.0
BF = jnp.bfloat16
F32 = jnp.float32


def dot(left, right):
    return jnp.dot(left, right, preferred_element_type=F32)


def dot_t(left, right):
    return lax.dot_general(left, right, (((0,), (0,)), ((), ())), preferred_element_type=F32)


def dot_rt(left, right):
    return lax.dot_general(left, right, (((1,), (1,)), ((), ())), preferred_element_type=F32)


def exact(spec, left, right):
    return jnp.einsum(
        spec, left, right, precision=lax.Precision.HIGHEST, preferred_element_type=F32
    )


def rms_gain(values, gain):
    return values * lax.rsqrt(jnp.mean(values * values, axis=-1, keepdims=True) + norm_eps) * gain


def gla_core(queries, keys, values, decays, mask, lower):
    length, width = queries.shape[1], queries.shape[3]
    total = exact("ts,nshd->nthd", lower, decays)
    middle = lax.stop_gradient(total[:, length // 2 - 1 : length // 2])
    query_up = queries * jnp.exp(total - middle)
    key_down = keys * jnp.exp(middle - total)
    scores = jnp.where(mask, exact("nthd,nshd->nhts", query_up, key_down), 0.0)
    return width ** (-0.5) * exact("nhts,nshd->nthd", scores, values)


def head_gate(core_out, gate_lin, head_gain):
    normed = (
        core_out
        * lax.rsqrt(jnp.mean(core_out * core_out, axis=-1, keepdims=True) + head_eps)
        * head_gain
    )
    gate_three = gate_lin.reshape(core_out.shape)
    return normed * gate_three * jax.nn.sigmoid(gate_three)


class Rows:
    def __init__(self):
        self.count = lax.axis_size("dp")
        self.direct = self.count <= 8
        self.outer = self.count // 2
        index = lax.axis_index("dp")
        self.z, self.x = index // 2, index % 2

    def slots(self):
        if not self.direct:
            return list(range(self.count))
        return [
            lax.rem(self.z - s + self.outer, self.outer) * 2 + (1 - self.x if b else self.x)
            for s in range(self.outer)
            for b in range(2)
        ]

    def relative(self, array, axis):
        if not self.direct:
            return array
        size = array.shape[axis] // self.count
        return jnp.concatenate(
            [lax.dynamic_slice_in_dim(array, slot * size, size, axis) for slot in self.slots()],
            axis=axis,
        )

    def pair(self, array):
        return lax.ppermute(array, "dp", [(i, i ^ 1) for i in range(self.count)])

    def shift(self, array, step):
        n = self.outer
        perm = [(i, (i // 2 + step) % n * 2 + i % 2) for i in range(self.count)]
        return lax.ppermute(array, "dp", perm)

    def gather(self, block, axis):
        if not self.direct:
            return lax.all_gather(block, "dp", axis=axis, tiled=True)
        line = [block] + [self.shift(block, s) for s in range(1, self.outer)]
        pieces = []
        for item in line:
            pieces += [item, self.pair(item)]
        return jnp.concatenate(pieces, axis=axis)

    def scatter(self, blocks):
        if not self.direct:
            stacked = jnp.stack([blocks(i).astype(F32) for i in range(self.count)])
            return lax.psum_scatter(stacked, "dp", scatter_dimension=0, tiled=False)
        sums = []
        for s in range(self.outer):
            got = self.pair(blocks(2 * s + 1).astype(BF))
            sums.append(blocks(2 * s).astype(F32) + got.astype(F32))
        total = sums[0]
        for s in range(1, self.outer):
            total = total + self.shift(sums[s].astype(BF), -s).astype(F32)
        return total


class Lanes:
    def __init__(self):
        self.count = lax.axis_size("mp")
        self.index = lax.axis_index("mp")

    def at(self, step):
        return lax.rem(self.index + step, self.count)

    def send(self, array, step):
        return lax.ppermute(
            array, "mp", [(i, (i + step) % self.count) for i in range(self.count)]
        )

    def own(self, array, step=0):
        size = array.shape[0] // self.count
        return lax.dynamic_slice_in_dim(array, self.at(step) * size, size, 0)

    def scatter(self, array):
        total = self.own(array).astype(F32)
        low = array.astype(BF)
        for step in range(1, self.count):
            total = total + self.send(self.own(low, step), step).astype(F32)
        return total

    def gather(self, chunk):
        pieces = [chunk] + [self.send(chunk, step) for step in range(1, self.count)]
        size = chunk.shape[0]
        result = jnp.zeros((size * self.count,) + chunk.shape[1:], chunk.dtype)
        for step, piece in enumerate(pieces):
            place = lax.rem(self.index - step + self.count, self.count) * size
            result = lax.dynamic_update_slice_in_dim(result, piece, place, 0)
        return result


def on_device(
    inputs,
    segment,
    norm_gain,
    w_query,
    w_key,
    w_value,
    w_gate_out,
    w_rank_in,
    w_rank_out,
    rank_bias,
    head_gain,
    w_output,
    ffn_gain,
    w_ffn_gate,
    w_ffn_up,
    w_ffn_down,
    cotangent,
):
    rows, lanes = Rows(), Lanes()
    micro, length, model = inputs.shape
    n_tok = micro * length
    heads_local = H // lanes.count
    key_cols, value_cols = w_query.shape[1], w_value.shape[1]

    small_parts = (norm_gain, ffn_gain, head_gain, rank_bias, w_rank_in, w_rank_out)
    small_sizes = [part.size for part in small_parts]
    small_total = sum(small_sizes)
    small_width = -(-small_total // 2048) * 2048
    flat = jnp.concatenate([part.reshape(-1) for part in small_parts])
    flat = jnp.pad(flat, (0, small_width - small_total)).reshape(1, 16, small_width // 16)
    small_rel = rows.gather(lanes.gather(flat)[None], 0)
    small_rel = small_rel.reshape(rows.count, lanes.count, small_width)
    small_abs = rows.relative(small_rel, 0)

    def small(source, which):
        start = sum(small_sizes[:which])
        return source[:, :, start : start + small_sizes[which]]

    gain_in = small(small_rel, 0).reshape(-1).astype(F32)
    gain_mid = small(small_rel, 1).reshape(-1).astype(F32)
    gain_head = small(small_abs, 2).reshape(-1).astype(F32)
    bias_all = small(small_abs, 3).reshape(-1)
    rank_in = small(small_rel, 4).reshape(model, -1)
    rank_out_all = small(small_abs, 5).reshape(-1, rank_in.shape[1])
    head_start = lanes.index * key_cols
    rank_out = lax.dynamic_slice_in_dim(rank_out_all, head_start, key_cols, 0)
    bias_local = lax.dynamic_slice_in_dim(bias_all, head_start, key_cols, 0).astype(F32)

    attn_mat = rows.gather(
        jnp.concatenate([w_query, w_key, w_value, w_gate_out, w_output], axis=1), 0
    )
    in_cols = 2 * key_cols + 2 * value_cols
    in_mat, out_mat = attn_mat[:, :in_cols], attn_mat[:, in_cols:]
    ffn_mat = rows.gather(jnp.stack([w_ffn_gate, w_ffn_up, w_ffn_down]), 1)
    full_gate, full_up, full_down = ffn_mat[0], ffn_mat[1], ffn_mat[2]

    tokens_low = rows.relative(inputs.reshape(n_tok, model), 1)
    dy_low = rows.relative(cotangent.reshape(n_tok, model), 1)
    tokens = tokens_low.astype(F32)
    own_tokens = lanes.own(tokens_low).astype(F32)
    own_dy = lanes.own(dy_low).astype(F32)
    normed_low = rms_gain(tokens, gain_in).astype(BF)
    projected = dot(normed_low, in_mat)
    qkv_low = projected[:, : in_cols - value_cols].astype(BF).astype(F32)
    gate_lin = projected[:, in_cols - value_cols :]
    rank_low = dot(normed_low, rank_in).astype(BF)
    logits = dot_rt(rank_low, rank_out) + bias_local
    decays = jax.nn.log_sigmoid(logits) / gate_divisor

    def heads(array):
        return array.reshape(micro, length, heads_local, -1)

    position = jnp.arange(length)
    lower_mask = position[:, None] >= position[None, :]
    same = segment[:, :, None] == segment[:, None, :]
    mask = (lower_mask[None] & same)[:, None]
    lower = lower_mask.astype(F32)

    def core(queries, keys, values, decay):
        return gla_core(queries, keys, values, decay, mask, lower)

    core_out, core_back = jax.vjp(
        core,
        heads(qkv_low[:, :key_cols]),
        heads(qkv_low[:, key_cols : 2 * key_cols]),
        heads(qkv_low[:, 2 * key_cols :]),
        heads(decays),
    )
    gated, gate_back = jax.vjp(head_gate, core_out, gate_lin, gain_head)
    gated_low = gated.reshape(n_tok, -1).astype(BF)
    own_attended = lanes.scatter(dot_rt(gated_low, out_mat))
    own_middle = own_tokens + own_attended
    own_mid, norm_mid_back = jax.vjp(rms_gain, own_middle, gain_mid)
    mid_low = lanes.gather(own_mid.astype(BF))
    d_hidden = dot(dy_low, full_down)
    gate_act = dot(mid_low, full_gate)
    up_act = dot(mid_low, full_up)
    sigma = jax.nn.sigmoid(gate_act)
    hidden_low = (gate_act * sigma * up_act).astype(BF)

    d_gate_low = (d_hidden * up_act * sigma * (1.0 + gate_act * (1.0 - sigma))).astype(BF)
    d_up_low = (d_hidden * gate_act * sigma).astype(BF)
    own_d_mid = lanes.scatter(dot_rt(d_gate_low, full_gate) + dot_rt(d_up_low, full_up))
    own_output = own_middle + lanes.scatter(dot_rt(hidden_low, full_down))
    grad_down = dot_t(dy_low, hidden_low).astype(BF)
    grad_gate = dot_t(mid_low, d_gate_low).astype(BF)
    grad_up = dot_t(mid_low, d_up_low).astype(BF)
    block = model // rows.count

    def ffn_block(slot):
        part = slice(slot * block, (slot + 1) * block)
        return jnp.stack([grad_gate[part], grad_up[part], grad_down[part]])

    ffn_grads = rows.scatter(ffn_block)
    own_d_middle, grad_gain_mid = norm_mid_back(own_d_mid)
    own_d_middle = own_dy + own_d_middle

    d_att_low = lanes.gather(own_d_middle.astype(BF))
    d_gated = dot(d_att_low, out_mat)
    d_core, d_gate_lin, grad_head = gate_back(heads(d_gated))
    d_queries, d_keys, d_values, d_decays = core_back(d_core)
    d_in_low = jnp.concatenate(
        [
            d_queries.reshape(n_tok, -1).astype(BF),
            d_keys.reshape(n_tok, -1).astype(BF),
            d_values.reshape(n_tok, -1).astype(BF),
            d_gate_lin.astype(BF),
        ],
        axis=1,
    )
    d_logit_low = (d_decays.reshape(n_tok, -1) * jax.nn.sigmoid(-logits) / gate_divisor).astype(BF)
    d_rank_low = dot(d_logit_low, rank_out).astype(BF)
    own_d_in = lanes.scatter(dot_rt(d_in_low, in_mat) + dot_rt(d_rank_low, rank_in))
    grad_in = dot_t(normed_low, d_in_low).astype(BF)
    grad_out = dot_t(d_att_low, gated_low).astype(BF)

    def attn_block(slot):
        part = slice(slot * block, (slot + 1) * block)
        return jnp.concatenate([grad_in[part], grad_out[part]], axis=1)

    attn_grads = rows.scatter(attn_block)
    _, norm_in_back = jax.vjp(rms_gain, own_tokens, gain_in)
    own_d_tokens, grad_gain_in = norm_in_back(own_d_in)
    own_input_grad = own_d_middle + own_d_tokens

    grad_rank_out = dot_t(d_logit_low, rank_low)
    grad_bias = jnp.sum(d_logit_low.astype(F32), axis=0)
    grad_rank_in = dot_t(normed_low, d_rank_low)
    rank_out_full = lax.dynamic_update_slice_in_dim(
        jnp.zeros(rank_out_all.shape, F32), grad_rank_out, head_start, 0
    )
    bias_full = lax.dynamic_update_slice_in_dim(
        jnp.zeros(bias_all.shape, F32), grad_bias, head_start, 0
    )

    def owners(array):
        return array.reshape(rows.count, lanes.count, -1)

    small_grads = jnp.concatenate(
        [
            owners(grad_gain_in),
            owners(grad_gain_mid),
            rows.relative(
                jnp.concatenate([owners(grad_head), owners(bias_full)], axis=2), 0
            ),
            owners(grad_rank_in),
            rows.relative(owners(rank_out_full), 0),
        ],
        axis=2,
    )
    small_grads = jnp.pad(small_grads, ((0, 0), (0, 0), (0, small_width - small_total)))
    small_sum = rows.scatter(lambda slot: small_grads[slot])
    small_own = lanes.scatter(small_sum).reshape(-1)

    def small_out(which, like):
        start = sum(small_sizes[:which])
        return small_own[start : start + small_sizes[which]].reshape(like.shape)

    output = rows.relative(lanes.gather(own_output.astype(BF)), 1)
    input_grad = rows.relative(lanes.gather(own_input_grad.astype(BF)), 1).astype(F32)
    kk, kv = key_cols, value_cols
    return (
        output.reshape(inputs.shape),
        input_grad.reshape(inputs.shape),
        small_out(0, norm_gain),
        attn_grads[:, :kk],
        attn_grads[:, kk : 2 * kk],
        attn_grads[:, 2 * kk : 2 * kk + kv],
        attn_grads[:, 2 * kk + kv : in_cols],
        small_out(4, w_rank_in),
        small_out(5, w_rank_out),
        small_out(3, rank_bias),
        small_out(2, head_gain),
        attn_grads[:, in_cols:],
        small_out(1, ffn_gain),
        ffn_grads[0],
        ffn_grads[1],
        ffn_grads[2],
    )


def solution(mesh):
    in_specs = (
        P(None, "dp", None),
        P(None, "dp"),
        P(("dp", "mp")),
        P("dp", "mp"),
        P("dp", "mp"),
        P("dp", "mp"),
        P("dp", "mp"),
        P(("dp", "mp"), None),
        P(("dp", "mp"), None),
        P(("dp", "mp")),
        P(("dp", "mp")),
        P("dp", "mp"),
        P(("dp", "mp")),
        P("dp", "mp"),
        P("dp", "mp"),
        P("dp", "mp"),
        P(None, "dp", None),
    )
    out_specs = (
        P(None, "dp", None),
        P(None, "dp", None),
        P(("dp", "mp")),
        P("dp", "mp"),
        P("dp", "mp"),
        P("dp", "mp"),
        P("dp", "mp"),
        P(("dp", "mp"), None),
        P(("dp", "mp"), None),
        P(("dp", "mp")),
        P(("dp", "mp")),
        P("dp", "mp"),
        P(("dp", "mp")),
        P("dp", "mp"),
        P("dp", "mp"),
        P("dp", "mp"),
    )
    return jax.shard_map(
        on_device, mesh=mesh, in_specs=in_specs, out_specs=out_specs, check_vma=False
    )
```

```python
import jax
import jax.numpy as jnp
from jax import lax
from jax.sharding import PartitionSpec as P

H = 4
norm_eps = 1e-06
head_eps = 0.1
gate_divisor = 16.0
BF = jnp.bfloat16
F32 = jnp.float32


def dot(left, right):
    return jnp.dot(left, right, preferred_element_type=F32)


def dot_t(left, right):
    return lax.dot_general(left, right, (((0,), (0,)), ((), ())), preferred_element_type=F32)


def dot_rt(left, right):
    return lax.dot_general(left, right, (((1,), (1,)), ((), ())), preferred_element_type=F32)


def exact(spec, left, right):
    return jnp.einsum(
        spec, left, right, precision=lax.Precision.HIGHEST, preferred_element_type=F32
    )


def rms_gain(values, gain):
    return values * lax.rsqrt(jnp.mean(values * values, axis=-1, keepdims=True) + norm_eps) * gain


def gla_core(queries, keys, values, decays, mask, lower):
    length, width = queries.shape[1], queries.shape[3]
    total = exact("ts,nshd->nthd", lower, decays)
    middle = lax.stop_gradient(total[:, length // 2 - 1 : length // 2])
    query_up = queries * jnp.exp(total - middle)
    key_down = keys * jnp.exp(middle - total)
    scores = jnp.where(mask, exact("nthd,nshd->nhts", query_up, key_down), 0.0)
    return width ** (-0.5) * exact("nhts,nshd->nthd", scores, values)


def head_gate(core_out, gate_lin, head_gain):
    normed = (
        core_out
        * lax.rsqrt(jnp.mean(core_out * core_out, axis=-1, keepdims=True) + head_eps)
        * head_gain
    )
    gate_three = gate_lin.reshape(core_out.shape)
    return normed * gate_three * jax.nn.sigmoid(gate_three)


def after(value, *earlier):
    return lax.optimization_barrier((value,) + earlier)[0]


class Rows:
    def __init__(self):
        self.count = lax.axis_size("dp")
        self.direct = self.count <= 8
        self.outer = self.count // 2
        index = lax.axis_index("dp")
        self.z, self.x = index // 2, index % 2

    def slots(self):
        if not self.direct:
            return list(range(self.count))
        return [
            lax.rem(self.z - s + self.outer, self.outer) * 2 + (1 - self.x if b else self.x)
            for s in range(self.outer)
            for b in range(2)
        ]

    def relative(self, array, axis):
        if not self.direct:
            return array
        size = array.shape[axis] // self.count
        return jnp.concatenate(
            [lax.dynamic_slice_in_dim(array, slot * size, size, axis) for slot in self.slots()],
            axis=axis,
        )

    def pair(self, array):
        return lax.ppermute(array, "dp", [(i, i ^ 1) for i in range(self.count)])

    def shift(self, array, step):
        n = self.outer
        perm = [(i, (i // 2 + step) % n * 2 + i % 2) for i in range(self.count)]
        return lax.ppermute(array, "dp", perm)

    def gather(self, block, earlier=()):
        if not self.direct:
            every = lax.all_gather(block, "dp", axis=0, tiled=False)
            return [every[i] for i in range(self.count)], [every]
        line = [block]
        for s in range(1, self.outer):
            gate = earlier[s - 1 : s] if len(earlier) >= s else ()
            line.append(self.shift(after(block, *gate), s))
        pieces, order = [], line[1:]
        for item in line:
            other = self.pair(item)
            pieces += [item, other]
            order.append(other)
        return pieces, order

    def pair_sums(self, blocks):
        if not self.direct:
            return [blocks(i).astype(F32) for i in range(self.count)], []
        sums, arrived = {}, []
        for s in list(range(1, self.outer)) + [0]:
            got = self.pair(blocks(2 * s + 1).astype(BF))
            sums[s] = blocks(2 * s).astype(F32) + got.astype(F32)
            if s:
                sums[s] = sums[s].astype(BF)
            arrived.append(sums[s])
        return [sums[s] for s in range(self.outer)], arrived

    def line_sum(self, sums):
        if not self.direct:
            return lax.psum_scatter(jnp.stack(sums), "dp", scatter_dimension=0), []
        arrived = [self.shift(sums[s], -s) for s in range(1, self.outer)]
        total = sums[0]
        for part in arrived:
            total = total + part.astype(F32)
        return total, arrived


class Lanes:
    def __init__(self):
        self.count = lax.axis_size("mp")
        self.index = lax.axis_index("mp")

    def at(self, step):
        return lax.rem(self.index + step, self.count)

    def send(self, array, step):
        return lax.ppermute(
            array, "mp", [(i, (i + step) % self.count) for i in range(self.count)]
        )

    def own(self, array, step=0):
        size = array.shape[0] // self.count
        return lax.dynamic_slice_in_dim(array, self.at(step) * size, size, 0)

    def scatter(self, array):
        total = self.own(array).astype(F32)
        low = array.astype(BF)
        for step in range(1, self.count):
            total = total + self.send(self.own(low, step), step).astype(F32)
        return total

    def gather(self, chunk):
        pieces = [chunk] + [self.send(chunk, step) for step in range(1, self.count)]
        size = chunk.shape[0]
        result = jnp.zeros((size * self.count,) + chunk.shape[1:], chunk.dtype)
        for step, piece in enumerate(pieces):
            place = lax.rem(self.index - step + self.count, self.count) * size
            result = lax.dynamic_update_slice_in_dim(result, piece, place, 0)
        return result


def on_device(
    inputs,
    segment,
    norm_gain,
    w_query,
    w_key,
    w_value,
    w_gate_out,
    w_rank_in,
    w_rank_out,
    rank_bias,
    head_gain,
    w_output,
    ffn_gain,
    w_ffn_gate,
    w_ffn_up,
    w_ffn_down,
    cotangent,
):
    rows, lanes = Rows(), Lanes()
    micro, length, model = inputs.shape
    n_tok = micro * length
    heads_local = H // lanes.count
    key_cols, value_cols = w_query.shape[1], w_value.shape[1]

    small_parts = (norm_gain, ffn_gain, head_gain, rank_bias, w_rank_in, w_rank_out)
    small_sizes = [part.size for part in small_parts]
    small_total = sum(small_sizes)
    small_width = -(-small_total // 2048) * 2048
    flat = jnp.concatenate([part.reshape(-1) for part in small_parts])
    flat = jnp.pad(flat, (0, small_width - small_total)).reshape(1, 16, small_width // 16)
    model_rows = w_query.shape[0]
    pack_cols = 2 * key_cols + 3 * value_cols
    small_rows = lanes.gather(flat).reshape(-1, pack_cols)
    attn_pieces, attn_order = rows.gather(
        jnp.concatenate(
            [
                jnp.concatenate([w_query, w_key, w_value, w_gate_out, w_output], axis=1),
                small_rows,
            ]
        )
    )
    small_rel = jnp.stack([piece[model_rows:] for piece in attn_pieces])
    small_rel = small_rel.reshape(rows.count, lanes.count, small_width)
    small_abs = rows.relative(small_rel, 0)

    def small(source, which):
        start = sum(small_sizes[:which])
        return source[:, :, start : start + small_sizes[which]]

    gain_in = small(small_rel, 0).reshape(-1).astype(F32)
    gain_mid = small(small_rel, 1).reshape(-1).astype(F32)
    gain_head = small(small_abs, 2).reshape(-1).astype(F32)
    bias_all = small(small_abs, 3).reshape(-1)
    rank_in = small(small_rel, 4).reshape(model, -1)
    rank_out_all = small(small_abs, 5).reshape(-1, rank_in.shape[1])
    head_start = lanes.index * key_cols
    rank_out = lax.dynamic_slice_in_dim(rank_out_all, head_start, key_cols, 0)
    bias_local = lax.dynamic_slice_in_dim(bias_all, head_start, key_cols, 0).astype(F32)

    attn_mat = jnp.concatenate([piece[:model_rows] for piece in attn_pieces])
    in_cols = 2 * key_cols + 2 * value_cols
    in_mat, out_mat = attn_mat[:, :in_cols], attn_mat[:, in_cols:]
    ffn_pieces, ffn_order = rows.gather(
        jnp.stack([w_ffn_gate, w_ffn_up, w_ffn_down]), attn_order
    )
    ffn_mat = jnp.concatenate(ffn_pieces, axis=1)
    full_gate, full_up, full_down = ffn_mat[0], ffn_mat[1], ffn_mat[2]

    tokens_low = rows.relative(inputs.reshape(n_tok, model), 1)
    dy_low = rows.relative(after(cotangent, attn_order[-1]).reshape(n_tok, model), 1)
    tokens = tokens_low.astype(F32)
    own_tokens = lanes.own(tokens_low).astype(F32)
    own_dy = lanes.own(dy_low).astype(F32)
    normed_low = rms_gain(tokens, gain_in).astype(BF)
    projected = after(dot(normed_low, in_mat), *ffn_order[:1])
    qkv_low = projected[:, : in_cols - value_cols].astype(BF).astype(F32)
    gate_lin = projected[:, in_cols - value_cols :]
    rank_low = dot(normed_low, rank_in).astype(BF)
    logits = dot_rt(rank_low, rank_out) + bias_local
    decays = jax.nn.log_sigmoid(logits) / gate_divisor

    def heads(array):
        return array.reshape(micro, length, heads_local, -1)

    position = jnp.arange(length)
    lower_mask = position[:, None] >= position[None, :]
    same = segment[:, :, None] == segment[:, None, :]
    mask = (lower_mask[None] & same)[:, None]
    lower = lower_mask.astype(F32)

    def core(queries, keys, values, decay):
        return gla_core(queries, keys, values, decay, mask, lower)

    core_out, core_back = jax.vjp(
        core,
        heads(qkv_low[:, :key_cols]),
        heads(qkv_low[:, key_cols : 2 * key_cols]),
        heads(qkv_low[:, 2 * key_cols :]),
        heads(decays),
    )
    gated, gate_back = jax.vjp(head_gate, core_out, gate_lin, gain_head)
    gated_low = after(gated.reshape(n_tok, -1).astype(BF), *ffn_order[1:2])
    own_attended = lanes.scatter(dot_rt(gated_low, out_mat))
    own_middle = own_tokens + own_attended
    own_mid, norm_mid_back = jax.vjp(rms_gain, own_middle, gain_mid)
    mid_low = lanes.gather(after(own_mid.astype(BF), *ffn_order[2:4]))
    d_hidden = dot(dy_low, full_down)
    gate_act = dot(mid_low, full_gate)
    up_act = dot(mid_low, full_up)
    sigma = jax.nn.sigmoid(gate_act)
    hidden_low = (gate_act * sigma * up_act).astype(BF)

    d_gate_low = (d_hidden * up_act * sigma * (1.0 + gate_act * (1.0 - sigma))).astype(BF)
    d_up_low = (d_hidden * gate_act * sigma).astype(BF)
    own_d_mid = lanes.scatter(dot_rt(d_gate_low, full_gate) + dot_rt(d_up_low, full_up))
    grad_down = dot_t(dy_low, hidden_low).astype(BF)
    grad_gate = dot_t(mid_low, d_gate_low).astype(BF)
    grad_up = dot_t(mid_low, d_up_low).astype(BF)
    block = model // rows.count

    def ffn_block(slot):
        part = slice(slot * block, (slot + 1) * block)
        return jnp.stack([grad_gate[part], grad_up[part], grad_down[part]])

    ffn_sums, ffn_pairs = rows.pair_sums(ffn_block)
    own_d_middle, grad_gain_mid = norm_mid_back(own_d_mid)
    own_d_middle = own_dy + own_d_middle

    d_att_low = after(lanes.gather(own_d_middle.astype(BF)), *ffn_pairs[:1])
    d_gated = dot(d_att_low, out_mat)
    d_core, d_gate_lin, grad_head = gate_back(heads(d_gated))
    d_core = after(d_core, *ffn_pairs[1:2])
    d_queries, d_keys, d_values, d_decays = core_back(d_core)
    d_in_low = jnp.concatenate(
        [
            d_queries.reshape(n_tok, -1).astype(BF),
            d_keys.reshape(n_tok, -1).astype(BF),
            d_values.reshape(n_tok, -1).astype(BF),
            d_gate_lin.astype(BF),
        ],
        axis=1,
    )
    d_logit_low = (d_decays.reshape(n_tok, -1) * jax.nn.sigmoid(-logits) / gate_divisor).astype(BF)
    d_rank_low = dot(d_logit_low, rank_out).astype(BF)
    own_d_in = lanes.scatter(dot_rt(d_in_low, in_mat) + dot_rt(d_rank_low, rank_in))
    ffn_grads, ffn_shifts = rows.line_sum(ffn_sums)
    grad_in = dot_t(normed_low, after(d_in_low, *ffn_pairs[2:], *ffn_shifts[:1])).astype(BF)
    grad_out = dot_t(d_att_low, gated_low).astype(BF)

    _, norm_in_back = jax.vjp(rms_gain, own_tokens, gain_in)
    own_d_tokens, grad_gain_in = norm_in_back(own_d_in)
    own_input_grad = own_d_middle + own_d_tokens

    grad_rank_out = dot_t(d_logit_low, rank_low)
    grad_bias = jnp.sum(d_logit_low.astype(F32), axis=0)
    grad_rank_in = dot_t(normed_low, d_rank_low)
    rank_out_full = lax.dynamic_update_slice_in_dim(
        jnp.zeros(rank_out_all.shape, F32), grad_rank_out, head_start, 0
    )
    bias_full = lax.dynamic_update_slice_in_dim(
        jnp.zeros(bias_all.shape, F32), grad_bias, head_start, 0
    )

    def owners(array):
        return array.reshape(rows.count, lanes.count, -1)

    small_grads = jnp.concatenate(
        [
            owners(grad_gain_in),
            owners(grad_gain_mid),
            rows.relative(
                jnp.concatenate([owners(grad_head), owners(bias_full)], axis=2), 0
            ),
            owners(grad_rank_in),
            rows.relative(owners(rank_out_full), 0),
        ],
        axis=2,
    )
    small_grads = jnp.pad(small_grads, ((0, 0), (0, 0), (0, small_width - small_total)))
    small_part = lanes.scatter(jnp.swapaxes(small_grads, 0, 1).astype(BF))[0]
    small_part = small_part.astype(BF).reshape(rows.count, -1, pack_cols)

    def attn_block(slot):
        part = slice(slot * block, (slot + 1) * block)
        mats = jnp.concatenate([grad_in[part], grad_out[part]], axis=1)
        return jnp.concatenate([mats, small_part[slot]])

    attn_sums, _ = rows.pair_sums(attn_block)
    attn_grads, _ = rows.line_sum(attn_sums)
    small_own = attn_grads[block:].reshape(-1)
    attn_grads = attn_grads[:block]
    late_hidden = after(hidden_low, own_d_in)
    own_output = own_middle + lanes.scatter(dot_rt(late_hidden, full_down))

    def small_out(which, like):
        start = sum(small_sizes[:which])
        return small_own[start : start + small_sizes[which]].reshape(like.shape)

    output = rows.relative(lanes.gather(own_output.astype(BF)), 1)
    input_grad = rows.relative(lanes.gather(own_input_grad.astype(BF)), 1).astype(F32)
    kk, kv = key_cols, value_cols
    return (
        output.reshape(inputs.shape),
        input_grad.reshape(inputs.shape),
        small_out(0, norm_gain),
        attn_grads[:, :kk],
        attn_grads[:, kk : 2 * kk],
        attn_grads[:, 2 * kk : 2 * kk + kv],
        attn_grads[:, 2 * kk + kv : in_cols],
        small_out(4, w_rank_in),
        small_out(5, w_rank_out),
        small_out(3, rank_bias),
        small_out(2, head_gain),
        attn_grads[:, in_cols:],
        small_out(1, ffn_gain),
        ffn_grads[0],
        ffn_grads[1],
        ffn_grads[2],
    )


def solution(mesh):
    in_specs = (
        P(None, "dp", None),
        P(None, "dp"),
        P(("dp", "mp")),
        P("dp", "mp"),
        P("dp", "mp"),
        P("dp", "mp"),
        P("dp", "mp"),
        P(("dp", "mp"), None),
        P(("dp", "mp"), None),
        P(("dp", "mp")),
        P(("dp", "mp")),
        P("dp", "mp"),
        P(("dp", "mp")),
        P("dp", "mp"),
        P("dp", "mp"),
        P("dp", "mp"),
        P(None, "dp", None),
    )
    out_specs = (
        P(None, "dp", None),
        P(None, "dp", None),
        P(("dp", "mp")),
        P("dp", "mp"),
        P("dp", "mp"),
        P("dp", "mp"),
        P("dp", "mp"),
        P(("dp", "mp"), None),
        P(("dp", "mp"), None),
        P(("dp", "mp")),
        P(("dp", "mp")),
        P("dp", "mp"),
        P(("dp", "mp")),
        P("dp", "mp"),
        P("dp", "mp"),
        P("dp", "mp"),
    )
    return jax.shard_map(
        on_device, mesh=mesh, in_specs=in_specs, out_specs=out_specs, check_vma=False
    )
```

```python
import jax
import jax.numpy as jnp
from jax import lax
from jax.sharding import PartitionSpec as P

H = 4
norm_eps = 1e-06
head_eps = 0.1
gate_divisor = 16.0
BF = jnp.bfloat16
F32 = jnp.float32


def dot(left, right):
    return jnp.dot(left, right, preferred_element_type=F32)


def dot_t(left, right):
    return lax.dot_general(left, right, (((0,), (0,)), ((), ())), preferred_element_type=F32)


def dot_rt(left, right):
    return lax.dot_general(left, right, (((1,), (1,)), ((), ())), preferred_element_type=F32)


def exact(spec, left, right):
    return jnp.einsum(
        spec, left, right, precision=lax.Precision.HIGHEST, preferred_element_type=F32
    )


def rms_gain(values, gain):
    return values * lax.rsqrt(jnp.mean(values * values, axis=-1, keepdims=True) + norm_eps) * gain


def gla_core(queries, keys, values, decays, mask, lower):
    length, width = queries.shape[1], queries.shape[3]
    total = exact("ts,nshd->nthd", lower, decays)
    middle = lax.stop_gradient(total[:, length // 2 - 1 : length // 2])
    query_up = queries * jnp.exp(total - middle)
    key_down = keys * jnp.exp(middle - total)
    scores = jnp.where(mask, exact("nthd,nshd->nhts", query_up, key_down), 0.0)
    return width ** (-0.5) * exact("nhts,nshd->nthd", scores, values)


def head_gate(core_out, gate_lin, head_gain):
    normed = (
        core_out
        * lax.rsqrt(jnp.mean(core_out * core_out, axis=-1, keepdims=True) + head_eps)
        * head_gain
    )
    gate_three = gate_lin.reshape(core_out.shape)
    return normed * gate_three * jax.nn.sigmoid(gate_three)


def after(value, *earlier):
    return lax.optimization_barrier((value,) + earlier)[0]


class Rows:
    def __init__(self):
        self.count = lax.axis_size("dp")
        self.direct = self.count <= 8
        self.outer = self.count // 2
        index = lax.axis_index("dp")
        self.z, self.x = index // 2, index % 2

    def slots(self):
        if not self.direct:
            return list(range(self.count))
        return [
            lax.rem(self.z - s + self.outer, self.outer) * 2 + (1 - self.x if b else self.x)
            for s in range(self.outer)
            for b in range(2)
        ]

    def relative(self, array, axis):
        if not self.direct:
            return array
        size = array.shape[axis] // self.count
        return jnp.concatenate(
            [lax.dynamic_slice_in_dim(array, slot * size, size, axis) for slot in self.slots()],
            axis=axis,
        )

    def pair(self, array):
        return lax.ppermute(array, "dp", [(i, i ^ 1) for i in range(self.count)])

    def shift(self, array, step):
        n = self.outer
        perm = [(i, (i // 2 + step) % n * 2 + i % 2) for i in range(self.count)]
        return lax.ppermute(array, "dp", perm)

    def gather(self, block, earlier=()):
        if not self.direct:
            every = lax.all_gather(block, "dp", axis=0, tiled=False)
            return [every[i] for i in range(self.count)], [every]
        line = [block]
        for s in range(1, self.outer):
            gate = earlier[s - 1 : s] if len(earlier) >= s else ()
            line.append(self.shift(after(block, *gate), s))
        pieces, order = [], line[1:]
        for item in line:
            other = self.pair(item)
            pieces += [item, other]
            order.append(other)
        return pieces, order

    def pair_sums(self, blocks):
        if not self.direct:
            return [blocks(i).astype(F32) for i in range(self.count)], []
        sums, arrived = {}, []
        for s in list(range(1, self.outer)) + [0]:
            got = self.pair(blocks(2 * s + 1).astype(BF))
            sums[s] = blocks(2 * s).astype(F32) + got.astype(F32)
            if s:
                sums[s] = sums[s].astype(BF)
            arrived.append(sums[s])
        return [sums[s] for s in range(self.outer)], arrived

    def line_sum(self, sums):
        if not self.direct:
            return lax.psum_scatter(jnp.stack(sums), "dp", scatter_dimension=0), []
        arrived = [self.shift(sums[s], -s) for s in range(1, self.outer)]
        total = sums[0]
        for part in arrived:
            total = total + part.astype(F32)
        return total, arrived


class Lanes:
    def __init__(self):
        self.count = lax.axis_size("mp")
        self.index = lax.axis_index("mp")

    def at(self, step):
        return lax.rem(self.index + step, self.count)

    def send(self, array, step):
        return lax.ppermute(
            array, "mp", [(i, (i + step) % self.count) for i in range(self.count)]
        )

    def own(self, array, step=0):
        size = array.shape[0] // self.count
        return lax.dynamic_slice_in_dim(array, self.at(step) * size, size, 0)

    def scatter(self, array):
        total = self.own(array).astype(F32)
        low = array.astype(BF)
        for step in range(1, self.count):
            total = total + self.send(self.own(low, step), step).astype(F32)
        return total

    def gather(self, chunk):
        pieces = [chunk] + [self.send(chunk, step) for step in range(1, self.count)]
        size = chunk.shape[0]
        result = jnp.zeros((size * self.count,) + chunk.shape[1:], chunk.dtype)
        for step, piece in enumerate(pieces):
            place = lax.rem(self.index - step + self.count, self.count) * size
            result = lax.dynamic_update_slice_in_dim(result, piece, place, 0)
        return result


def on_device(
    inputs,
    segment,
    norm_gain,
    w_query,
    w_key,
    w_value,
    w_gate_out,
    w_rank_in,
    w_rank_out,
    rank_bias,
    head_gain,
    w_output,
    ffn_gain,
    w_ffn_gate,
    w_ffn_up,
    w_ffn_down,
    cotangent,
):
    rows, lanes = Rows(), Lanes()
    micro, length, model = inputs.shape
    n_tok = micro * length
    heads_local = H // lanes.count
    key_cols, value_cols = w_query.shape[1], w_value.shape[1]

    small_parts = (norm_gain, ffn_gain, head_gain, rank_bias, w_rank_in, w_rank_out)
    small_sizes = [part.size for part in small_parts]
    small_total = sum(small_sizes)
    small_width = -(-small_total // 2048) * 2048
    flat = jnp.concatenate([part.reshape(-1) for part in small_parts])
    flat = jnp.pad(flat, (0, small_width - small_total)).reshape(1, 16, small_width // 16)
    model_rows = w_query.shape[0]
    pack_cols = 2 * key_cols + 3 * value_cols
    small_rows = lanes.gather(flat).reshape(-1, pack_cols)
    attn_pieces, attn_order = rows.gather(
        jnp.concatenate(
            [
                jnp.concatenate([w_query, w_key, w_value, w_gate_out, w_output], axis=1),
                small_rows,
            ]
        )
    )
    small_rel = jnp.stack([piece[model_rows:] for piece in attn_pieces])
    small_rel = small_rel.reshape(rows.count, lanes.count, small_width)
    small_abs = rows.relative(small_rel, 0)

    def small(source, which):
        start = sum(small_sizes[:which])
        return source[:, :, start : start + small_sizes[which]]

    gain_in = small(small_rel, 0).reshape(-1).astype(F32)
    gain_mid = small(small_rel, 1).reshape(-1).astype(F32)
    gain_head = small(small_abs, 2).reshape(-1).astype(F32)
    bias_all = small(small_abs, 3).reshape(-1)
    rank_in = small(small_rel, 4).reshape(model, -1)
    rank_out_all = small(small_abs, 5).reshape(-1, rank_in.shape[1])
    head_start = lanes.index * key_cols
    rank_out = lax.dynamic_slice_in_dim(rank_out_all, head_start, key_cols, 0)
    bias_local = lax.dynamic_slice_in_dim(bias_all, head_start, key_cols, 0).astype(F32)

    attn_mat = jnp.concatenate([piece[:model_rows] for piece in attn_pieces])
    in_cols = 2 * key_cols + 2 * value_cols
    in_mat, out_mat = attn_mat[:, :in_cols], attn_mat[:, in_cols:]
    ffn_pieces, ffn_order = rows.gather(
        jnp.stack([w_ffn_gate, w_ffn_up, w_ffn_down])
    )
    ffn_mat = jnp.concatenate(ffn_pieces, axis=1)
    full_gate, full_up, full_down = ffn_mat[0], ffn_mat[1], ffn_mat[2]

    tokens_low = rows.relative(inputs.reshape(n_tok, model), 1)
    dy_low = rows.relative(cotangent.reshape(n_tok, model), 1)
    tokens = tokens_low.astype(F32)
    own_tokens = lanes.own(tokens_low).astype(F32)
    own_dy = lanes.own(dy_low).astype(F32)
    normed_low = rms_gain(tokens, gain_in).astype(BF)
    projected = dot(normed_low, in_mat)
    qkv_low = projected[:, : in_cols - value_cols].astype(BF).astype(F32)
    gate_lin = projected[:, in_cols - value_cols :]
    rank_low = dot(normed_low, rank_in).astype(BF)
    logits = dot_rt(rank_low, rank_out) + bias_local
    decays = jax.nn.log_sigmoid(logits) / gate_divisor

    def heads(array):
        return array.reshape(micro, length, heads_local, -1)

    position = jnp.arange(length)
    lower_mask = position[:, None] >= position[None, :]
    same = segment[:, :, None] == segment[:, None, :]
    mask = (lower_mask[None] & same)[:, None]
    lower = lower_mask.astype(F32)

    def core(queries, keys, values, decay):
        return gla_core(queries, keys, values, decay, mask, lower)

    core_out, core_back = jax.vjp(
        core,
        heads(qkv_low[:, :key_cols]),
        heads(qkv_low[:, key_cols : 2 * key_cols]),
        heads(qkv_low[:, 2 * key_cols :]),
        heads(decays),
    )
    gated, gate_back = jax.vjp(head_gate, core_out, gate_lin, gain_head)
    gated_low = gated.reshape(n_tok, -1).astype(BF)
    own_attended = lanes.scatter(dot_rt(gated_low, out_mat))
    own_middle = own_tokens + own_attended
    own_mid, norm_mid_back = jax.vjp(rms_gain, own_middle, gain_mid)
    mid_low = lanes.gather(own_mid.astype(BF))
    d_hidden = dot(dy_low, full_down)
    gate_act = dot(mid_low, full_gate)
    up_act = dot(mid_low, full_up)
    sigma = jax.nn.sigmoid(gate_act)
    hidden_low = (gate_act * sigma * up_act).astype(BF)

    d_gate_low = (d_hidden * up_act * sigma * (1.0 + gate_act * (1.0 - sigma))).astype(BF)
    d_up_low = (d_hidden * gate_act * sigma).astype(BF)
    own_d_mid = lanes.scatter(dot_rt(d_gate_low, full_gate) + dot_rt(d_up_low, full_up))
    grad_down = dot_t(dy_low, hidden_low).astype(BF)
    grad_gate = dot_t(mid_low, d_gate_low).astype(BF)
    grad_up = dot_t(mid_low, d_up_low).astype(BF)
    block = model // rows.count

    def ffn_block(slot):
        part = slice(slot * block, (slot + 1) * block)
        return jnp.stack([grad_gate[part], grad_up[part], grad_down[part]])

    ffn_sums, ffn_pairs = rows.pair_sums(ffn_block)
    own_d_middle, grad_gain_mid = norm_mid_back(own_d_mid)
    own_d_middle = own_dy + own_d_middle

    d_att_low = lanes.gather(own_d_middle.astype(BF))
    d_gated = dot(d_att_low, out_mat)
    d_core, d_gate_lin, grad_head = gate_back(heads(d_gated))
    d_core = after(d_core, *ffn_pairs[:1])
    d_queries, d_keys, d_values, d_decays = core_back(d_core)
    d_in_low = jnp.concatenate(
        [
            d_queries.reshape(n_tok, -1).astype(BF),
            d_keys.reshape(n_tok, -1).astype(BF),
            d_values.reshape(n_tok, -1).astype(BF),
            d_gate_lin.astype(BF),
        ],
        axis=1,
    )
    d_logit_low = (d_decays.reshape(n_tok, -1) * jax.nn.sigmoid(-logits) / gate_divisor).astype(BF)
    d_rank_low = dot(d_logit_low, rank_out).astype(BF)
    own_d_in = lanes.scatter(dot_rt(d_in_low, in_mat) + dot_rt(d_rank_low, rank_in))
    ffn_grads, ffn_shifts = rows.line_sum(ffn_sums)
    grad_in = dot_t(normed_low, after(d_in_low, *ffn_pairs[1:3])).astype(BF)
    grad_out = dot_t(d_att_low, gated_low).astype(BF)

    _, norm_in_back = jax.vjp(rms_gain, own_tokens, gain_in)
    own_d_tokens, grad_gain_in = norm_in_back(own_d_in)
    own_input_grad = own_d_middle + own_d_tokens

    grad_rank_out = dot_t(d_logit_low, rank_low)
    grad_bias = jnp.sum(d_logit_low.astype(F32), axis=0)
    grad_rank_in = dot_t(normed_low, d_rank_low)
    rank_out_full = lax.dynamic_update_slice_in_dim(
        jnp.zeros(rank_out_all.shape, F32), grad_rank_out, head_start, 0
    )
    bias_full = lax.dynamic_update_slice_in_dim(
        jnp.zeros(bias_all.shape, F32), grad_bias, head_start, 0
    )

    def owners(array):
        return array.reshape(rows.count, lanes.count, -1)

    small_grads = jnp.concatenate(
        [
            owners(grad_gain_in),
            owners(grad_gain_mid),
            rows.relative(
                jnp.concatenate([owners(grad_head), owners(bias_full)], axis=2), 0
            ),
            owners(grad_rank_in),
            rows.relative(owners(rank_out_full), 0),
        ],
        axis=2,
    )
    small_grads = jnp.pad(small_grads, ((0, 0), (0, 0), (0, small_width - small_total)))
    small_part = lanes.scatter(jnp.swapaxes(small_grads, 0, 1).astype(BF))[0]
    small_part = small_part.astype(BF).reshape(rows.count, -1, pack_cols)

    def attn_block(slot):
        part = slice(slot * block, (slot + 1) * block)
        mats = jnp.concatenate([grad_in[part], grad_out[part]], axis=1)
        return jnp.concatenate([mats, small_part[slot]])

    attn_sums, _ = rows.pair_sums(attn_block)
    attn_grads, _ = rows.line_sum(attn_sums)
    small_own = attn_grads[block:].reshape(-1)
    attn_grads = attn_grads[:block]
    late_hidden = after(hidden_low, own_d_in)
    own_output = own_middle + lanes.scatter(dot_rt(late_hidden, full_down))

    def small_out(which, like):
        start = sum(small_sizes[:which])
        return small_own[start : start + small_sizes[which]].reshape(like.shape)

    output = rows.relative(lanes.gather(own_output.astype(BF)), 1)
    input_grad = rows.relative(lanes.gather(own_input_grad.astype(BF)), 1).astype(F32)
    kk, kv = key_cols, value_cols
    return (
        output.reshape(inputs.shape),
        input_grad.reshape(inputs.shape),
        small_out(0, norm_gain),
        attn_grads[:, :kk],
        attn_grads[:, kk : 2 * kk],
        attn_grads[:, 2 * kk : 2 * kk + kv],
        attn_grads[:, 2 * kk + kv : in_cols],
        small_out(4, w_rank_in),
        small_out(5, w_rank_out),
        small_out(3, rank_bias),
        small_out(2, head_gain),
        attn_grads[:, in_cols:],
        small_out(1, ffn_gain),
        ffn_grads[0],
        ffn_grads[1],
        ffn_grads[2],
    )


def solution(mesh):
    in_specs = (
        P(None, "dp", None),
        P(None, "dp"),
        P(("dp", "mp")),
        P("dp", "mp"),
        P("dp", "mp"),
        P("dp", "mp"),
        P("dp", "mp"),
        P(("dp", "mp"), None),
        P(("dp", "mp"), None),
        P(("dp", "mp")),
        P(("dp", "mp")),
        P("dp", "mp"),
        P(("dp", "mp")),
        P("dp", "mp"),
        P("dp", "mp"),
        P("dp", "mp"),
        P(None, "dp", None),
    )
    out_specs = (
        P(None, "dp", None),
        P(None, "dp", None),
        P(("dp", "mp")),
        P("dp", "mp"),
        P("dp", "mp"),
        P("dp", "mp"),
        P("dp", "mp"),
        P(("dp", "mp"), None),
        P(("dp", "mp"), None),
        P(("dp", "mp")),
        P(("dp", "mp")),
        P("dp", "mp"),
        P(("dp", "mp")),
        P("dp", "mp"),
        P("dp", "mp"),
        P("dp", "mp"),
    )
    return jax.shard_map(
        on_device, mesh=mesh, in_specs=in_specs, out_specs=out_specs, check_vma=False
    )
```
